32 devices in a mesh: dp: 8 (over z, x), tensor: 4 (over y, core).
Axes of the slice: x: 2, y: 2, z: 4, core: 2. Of those that a mesh axis runs over, the one named last changes fastest.
Arguments:
- tokens: bfloat16 [16, 1024, 1024], P('dp', 'tensor'), may hold values from -6 to 6
- lengths: int32 [16, 4], P('dp'), may hold values from 60 to 800, as said below
- ln_attn: bfloat16 [1024], P('dp'), may hold values from 0.099609375 to 1.8984375
- w_query: bfloat16 [1024, 1024], P('dp', 'tensor'), may hold values from -0.1875 to 0.1875
- w_key: bfloat16 [1024, 512], P('dp', 'tensor'), may hold values from -0.1875 to 0.1875
- w_value: bfloat16 [1024, 512], P('dp', 'tensor'), may hold values from -0.1875 to 0.1875
- q_gain: bfloat16 [64], P('dp'), may hold values from 0.099609375 to 1.8984375
- k_gain: bfloat16 [64], P('dp'), may hold values from 0.099609375 to 1.8984375
- w_out: bfloat16 [1024, 1024], P('tensor', 'dp'), may hold values from -1.5 to 1.5
- ln_ffn: bfloat16 [1024], P('dp'), may hold values from 0.099609375 to 1.8984375
- w_gate: bfloat16 [1024, 4608], P('dp', 'tensor'), may hold values from -0.1875 to 0.1875
- w_up: bfloat16 [1024, 4608], P('dp', 'tensor'), may hold values from -0.1875 to 0.1875
- w_down: bfloat16 [4608, 1024], P('tensor', 'dp'), may hold values from -0.09375 to 0.09375
- out_grad: bfloat16 [16, 1024, 1024], P('dp', 'tensor'), may hold values from -6 to 6
Outputs:
- block_out: bfloat16 [16, 1024, 1024], P('dp', 'tensor')
- tokens_grad: float32 [16, 1024, 1024], P('dp', 'tensor')
- ln_attn_grad: float32 [1024], P('dp')
- w_query_grad: float32 [1024, 1024], P('dp', 'tensor')
- w_key_grad: float32 [1024, 512], P('dp', 'tensor')
- w_value_grad: float32 [1024, 512], P('dp', 'tensor')
- q_gain_grad: float32 [64], P('dp')
- k_gain_grad: float32 [64], P('dp')
- w_out_grad: float32 [1024, 1024], P('tensor', 'dp')
- ln_ffn_grad: float32 [1024], P('dp')
- w_gate_grad: float32 [1024, 4608], P('dp', 'tensor')
- up_weight_gradient: float32 [1024, 4608], P('dp', 'tensor')
- w_down_grad: float32 [4608, 1024], P('tensor', 'dp')
The draws below stay inside these ranges and needn't reach their ends.
Inputs may be any that keep to these rules, and one draw needn't show every extreme that they name: Row s lists the lengths of the 4 documents packed into sequence s, in order; each row sums to 1024, each document has at least 60 tokens, and exactly one document of each row has 800 tokens.
All inputs are finite; a program needn't handle non-finite values.
Results may differ from the reference program's by a relative error of at most 0.019.
Values may be sent and summed in bfloat16 or wider, within the bound.
A program may use at most 192 MiB of HBM per device.

```python
import math
import jax
import jax.numpy as jnp
from jax import lax

D = 1024
HEADS = 16
KV_HEADS = 8
HEAD_DIM = 64
FF = 4608
LEN = 1024
DOCS = 4
DOC_MOST = 800
DOC_LEAST = 60
SEQUENCES = 16


def draw_lengths(key, part):
    key = jax.random.fold_in(key, 11)
    spare = LEN - DOC_MOST - (DOCS - 1) * DOC_LEAST

    def one_row(row_key):
        pick_key, cut_key = jax.random.split(row_key)
        cuts = jnp.sort(jax.random.randint(cut_key, (DOCS - 2,), 0, spare + 1)).astype(jnp.int32)
        bounds = jnp.concatenate([jnp.zeros((1,), jnp.int32), cuts, jnp.full((1,), spare, jnp.int32)])
        others = (bounds[1:] - bounds[:-1] + DOC_LEAST).astype(jnp.int32)
        longest = jax.random.randint(pick_key, (), 0, DOCS).astype(jnp.int32)
        slots = jnp.arange(DOCS, dtype=jnp.int32)
        left_side = jnp.concatenate([others, jnp.zeros((1,), jnp.int32)])
        right_side = jnp.concatenate([jnp.zeros((1,), jnp.int32), others])
        return jnp.where(slots == longest, DOC_MOST, jnp.where(slots < longest, left_side, right_side)).astype(jnp.int32)
    return jax.vmap(one_row)(jax.random.split(key, SEQUENCES))


def strengthened(values, rng, source, target, shards_of, factor):
    owner, partner = [(jnp.arange(values.shape[axis_at]) // (values.shape[axis_at] // shards_of)).reshape([-1 if axis == axis_at else 1 for axis in range(values.ndim)]) for axis_at in (source, target)]
    chosen = jax.random.permutation(rng, shards_of)[partner]
    strong = (owner == chosen) | (owner == (partner + shards_of // 2) % shards_of)
    return jnp.where(strong, factor * values, values)


def shard_levels(rng, dims, shards, low, top_value):
    def one(axis_at, parts):
        draws = jax.random.uniform(jax.random.fold_in(jax.random.fold_in(rng, 6), axis_at), (parts,), jnp.float32, low / len(shards), top_value / len(shards))
        return jnp.repeat(jnp.exp(draws), dims[axis_at] // parts).reshape((-1,) + (1,) * (len(dims) - axis_at - 1))

    gain = one(*shards[0])
    for cut in shards[1:]:
        gain = gain * one(*cut)
    return gain


def gaussian(own_key, dims, width, bound, pieces=(), kind=jnp.bfloat16):
    values = width * jax.random.normal(own_key, dims, jnp.float32)
    if pieces:
        values = values * shard_levels(own_key, dims, pieces, -0.22, 0.18)
    return jnp.clip(values, -bound, bound).astype(kind)


def heavy_noise(stream_key, shape, spread, reach, pieces, heavy, held_as=jnp.bfloat16):
    entries = spread * jax.random.normal(stream_key, shape, jnp.float32)
    if pieces:
        entries = entries * shard_levels(stream_key, shape, pieces, -0.22, 0.18)
    return jnp.clip(strengthened(entries, jax.random.fold_in(stream_key, 3), *heavy), -reach, reach).astype(held_as)


def setup_inputs(seed: int = 0) -> dict:
    streams_of = jax.random.split(jax.random.key(seed), 15)
    return {
        "tokens": heavy_noise(streams_of[0], (SEQUENCES, LEN, D), 1.0, 6.0, ((0, 8), (1, 4)), (0, 2, 8, 2.0)),
        "lengths": draw_lengths(jax.random.fold_in(streams_of[14], 71), 0),
        "ln_attn": jnp.clip(1.0 + 0.18 * jax.random.normal(streams_of[2], (D,), jnp.float32), 0.099609375, 1.8984375).astype(jnp.bfloat16),
        "w_query": gaussian(streams_of[3], (D, HEADS * HEAD_DIM), D ** -0.5, 0.1875, ((0, 8), (1, 4))),
        "w_key": gaussian(streams_of[4], (D, KV_HEADS * HEAD_DIM), D ** -0.5, 0.1875, ((0, 8), (1, 4))),
        "w_value": gaussian(streams_of[5], (D, KV_HEADS * HEAD_DIM), D ** -0.5, 0.1875, ((0, 8), (1, 4))),
        "q_gain": jnp.clip(1.0 + 0.18 * jax.random.normal(streams_of[6], (HEAD_DIM,), jnp.float32), 0.099609375, 1.8984375).astype(jnp.bfloat16),
        "k_gain": jnp.clip(1.0 + 0.18 * jax.random.normal(streams_of[7], (HEAD_DIM,), jnp.float32), 0.099609375, 1.8984375).astype(jnp.bfloat16),
        "w_out": gaussian(streams_of[8], (HEADS * HEAD_DIM, D), (HEADS * HEAD_DIM // 64) ** -0.5, 1.5, ((0, 4), (1, 8))),
        "ln_ffn": jnp.clip(1.0 + 0.18 * jax.random.normal(streams_of[9], (D,), jnp.float32), 0.099609375, 1.8984375).astype(jnp.bfloat16),
        "w_gate": gaussian(streams_of[10], (D, FF), D ** -0.5, 0.1875, ((0, 8), (1, 4))),
        "w_up": gaussian(streams_of[11], (D, FF), D ** -0.5, 0.1875, ((0, 8), (1, 4))),
        "w_down": gaussian(streams_of[12], (FF, D), FF ** -0.5, 0.09375, ((0, 4), (1, 8))),
        "out_grad": heavy_noise(streams_of[13], (SEQUENCES, LEN, D), 1.0, 6.0, ((0, 8), (1, 4)), (0, 2, 8, 2.0)),
    }


@jax.custom_vjp
def low(v):
    return lax.optimization_barrier(v.astype(jnp.bfloat16)).astype(jnp.float32)

@jax.custom_vjp
def low_back(v):
    return v

def low_keep(v):
    return (low(v), None)

def low_pass(kept, grad):
    return (grad,)

def back_keep(v):
    return (v, None)

def back_low(kept, grad):
    return (low(grad),)
low.defvjp(low_keep, low_pass)
low_back.defvjp(back_keep, back_low)
EPSILON = 1e-05
THETA = 1000000.0
MASKED = -1e+30
TOP_PRECISION = lax.Precision.HIGHEST

def rms_scale(values, gain_vec):
    return values * lax.rsqrt(lax.optimization_barrier(jnp.mean(values * values, axis=-1, keepdims=True)) + EPSILON) * gain_vec

def doc_tables(lengths, seq_len):
    doc_ends = jnp.cumsum(lengths, axis=-1, dtype=jnp.int32)
    doc_starts = (doc_ends - lengths).astype(jnp.int32)
    positions = jnp.arange(seq_len, dtype=jnp.int32)
    doc_ids = lax.optimization_barrier(jnp.sum((positions[None, :, None] >= doc_ends[:, None, :]).astype(jnp.int32), axis=-1, dtype=jnp.int32))
    numbers = jnp.arange(lengths.shape[-1], dtype=jnp.int32)
    opening = lax.optimization_barrier(jnp.sum(jnp.where(doc_ids[:, :, None] == numbers[None, None, :], doc_starts[:, None, :], 0), axis=-1, dtype=jnp.int32))
    return (doc_ids, (positions[None, :] - opening).astype(jnp.int32))

def rotary(values, positions):
    half_dim = values.shape[-1] // 2
    freq_rate = jnp.power(THETA, -2.0 * jnp.arange(half_dim, dtype=jnp.float32) / values.shape[-1])
    angles = positions.astype(jnp.float32)[:, :, None, None] * freq_rate
    cosine = jnp.cos(angles)
    sine_part = jnp.sin(angles)
    front_half = values[..., :half_dim]
    back_half = values[..., half_dim:]
    return jnp.concatenate([front_half * cosine - back_half * sine_part, back_half * cosine + front_half * sine_part], axis=-1)

def allowed_mask(doc_ids):
    places = jnp.arange(doc_ids.shape[0], dtype=jnp.int32)
    return (doc_ids[:, None] == doc_ids[None, :]) & (places[None, :] <= places[:, None])

def product(matmul_operand, weight_matrix):
    return jnp.einsum('xpo,oh->xph', matmul_operand, weight_matrix, precision=TOP_PRECISION, preferred_element_type=jnp.float32)

def attend_sequence(packed):
    queries, key_rows, value_rows, doc_ids = packed
    seq_len, heads, head_dim = queries.shape
    key_value_heads = key_rows.shape[1]
    grouped = queries.reshape(seq_len, key_value_heads, heads // key_value_heads, head_dim)
    scores = jnp.einsum('qkgd,tkd->kgqt', grouped, key_rows, precision=TOP_PRECISION, preferred_element_type=jnp.float32)
    scores = low_back(scores * head_dim ** (-0.5))
    scores = jnp.where(allowed_mask(doc_ids), scores, MASKED)
    row_max = lax.optimization_barrier(jnp.max(scores, axis=-1, keepdims=True))
    exp_scores = jnp.exp(scores - row_max)
    probs = low(exp_scores / lax.optimization_barrier(jnp.sum(exp_scores, axis=-1, keepdims=True)))
    mixture = jnp.einsum('kgqt,tkd->qkgd', probs, value_rows, precision=TOP_PRECISION, preferred_element_type=jnp.float32)
    return mixture.reshape(seq_len, heads * head_dim)

def block_forward(inputs, ln_attn, w_query, w_key, w_value, q_gain, k_gain, w_out, ln_ffn, w_gate, w_up, w_down, doc_ids, positions):
    seq_count, seq_len = (inputs.shape[0], inputs.shape[1])
    head_dim = q_gain.shape[0]
    normed = low(rms_scale(inputs, ln_attn))
    query_raw = low_back(product(normed, w_query)).reshape(seq_count, seq_len, -1, head_dim)
    key_raw = low_back(product(normed, w_key)).reshape(seq_count, seq_len, -1, head_dim)
    queries = low(rotary(rms_scale(query_raw, q_gain), positions))
    key_rows = low(rotary(rms_scale(key_raw, k_gain), positions))
    value_rows = low(low_back(product(normed, w_value))).reshape(seq_count, seq_len, -1, head_dim)
    mixture = lax.map(jax.checkpoint(attend_sequence), (queries, key_rows, value_rows, doc_ids))
    mixture = low(low_back(mixture))
    mid_stream = inputs + low_back(product(mixture, w_out))
    normed_mid = low(rms_scale(mid_stream, ln_ffn))
    gate_proj = low_back(product(normed_mid, w_gate))
    up_proj = low_back(product(normed_mid, w_up))
    hidden = low(jax.nn.silu(gate_proj) * up_proj)
    return mid_stream + product(hidden, w_down)

def reference(tokens, lengths, ln_attn, w_query, w_key, w_value, q_gain, k_gain, w_out, ln_ffn, w_gate, w_up, w_down, out_grad):
    doc_ids, positions = doc_tables(lengths, LEN)
    weights = tuple((array.astype(jnp.float32) for array in (ln_attn, w_query, w_key, w_value, q_gain, k_gain, w_out, ln_ffn, w_gate, w_up, w_down)))
    group_size = math.gcd(SEQUENCES, 4)
    step_count = SEQUENCES // group_size

    def regroup(array):
        return array.reshape((step_count, group_size) + array.shape[1:])

    def group_stride(totals, packed):
        inputs, cotangent, group_ids, group_places = packed

        def forward(block_in, *params):
            return block_forward(block_in, *params, group_ids, group_places)
        result, pullback = jax.vjp(forward, inputs.astype(jnp.float32), *weights)
        gradients = pullback(cotangent.astype(jnp.float32))
        running = tuple((total_now + gradient_term for total_now, gradient_term in zip(totals, gradients[1:])))
        return (running, (result.astype(jnp.bfloat16), gradients[0]))
    initial = tuple((jnp.zeros(array.shape, jnp.float32) for array in weights))
    totals, (outputs, input_grads) = lax.scan(group_stride, initial, (regroup(tokens), regroup(out_grad), regroup(doc_ids), regroup(positions)))
    return (outputs.reshape(tokens.shape), input_grads.reshape(tokens.shape), totals[0], totals[1], totals[2], totals[3], totals[4], totals[5], totals[6], totals[7], totals[8], totals[9], totals[10])
```

```python
import jax
import jax.numpy as jnp
from jax import lax
from jax.sharding import PartitionSpec as P

EPSILON = 1e-05
THETA = 1000000.0
MASKED = -1e30


def rms_scale(values, gain_vec):
    return (
        values * lax.rsqrt(jnp.mean(values * values, axis=-1, keepdims=True) + EPSILON) * gain_vec
    )


def doc_tables(lengths, seq_len):
    doc_ends = jnp.cumsum(lengths, axis=-1, dtype=jnp.int32)
    doc_starts = doc_ends - lengths
    positions = jnp.arange(seq_len, dtype=jnp.int32)
    doc_ids = jnp.sum(
        (positions[None, :, None] >= doc_ends[:, None, :]).astype(jnp.int32),
        axis=-1,
        dtype=jnp.int32,
    )
    numbers = jnp.arange(lengths.shape[-1], dtype=jnp.int32)
    opening = jnp.sum(
        jnp.where(doc_ids[:, :, None] == numbers[None, None, :], doc_starts[:, None, :], 0),
        axis=-1,
        dtype=jnp.int32,
    )
    return (doc_ids, positions[None, :] - opening)


def rotary(values, positions):
    half_dim = values.shape[-1] // 2
    freq_rate = jnp.power(THETA, -2.0 * jnp.arange(half_dim, dtype=jnp.float32) / values.shape[-1])
    angles = positions.astype(jnp.float32)[:, :, None, None] * freq_rate
    cosine = jnp.cos(angles)
    sine_part = jnp.sin(angles)
    front_half = values[..., :half_dim]
    back_half = values[..., half_dim:]
    return jnp.concatenate(
        [front_half * cosine - back_half * sine_part, back_half * cosine + front_half * sine_part],
        axis=-1,
    )


def allowed_mask(doc_ids):
    places = jnp.arange(doc_ids.shape[0], dtype=jnp.int32)
    return (doc_ids[:, None] == doc_ids[None, :]) & (places[None, :] <= places[:, None])


def project(matmul_operand, weight_matrix):
    return jnp.einsum(
        "xpo,oh->xph", matmul_operand, weight_matrix, preferred_element_type=jnp.float32
    )


def project_back(gradient_term, weight_matrix):
    return jnp.einsum(
        "yhp,np->yhn", gradient_term, weight_matrix, preferred_element_type=jnp.float32
    )


def weight_grad(matmul_operand, gradient_term):
    return jnp.einsum(
        "wba,wbh->ah", matmul_operand, gradient_term, preferred_element_type=jnp.float32
    )


def score_block(queries, key_rows, doc_ids):
    seq_len, heads, head_dim = queries.shape
    key_value_heads = key_rows.shape[1]
    grouped = queries.reshape(seq_len, key_value_heads, heads // key_value_heads, head_dim)
    scores = jnp.einsum(
        "qkgd,tkd->kgqt", grouped, key_rows, preferred_element_type=jnp.float32
    ) * head_dim ** (-0.5)
    return (grouped, jnp.where(allowed_mask(doc_ids), scores, MASKED))


def attend_forward(packed):
    queries, key_rows, value_rows, doc_ids = packed
    seq_len = queries.shape[0]
    grouped, scores = score_block(queries, key_rows, doc_ids)
    row_max = jnp.max(scores, axis=-1, keepdims=True)
    exp_scores = jnp.exp(scores - row_max)
    row_total = jnp.sum(exp_scores, axis=-1, keepdims=True)
    probs = (exp_scores / row_total).astype(jnp.bfloat16)
    mixture = jnp.einsum("kgqt,tkd->qkgd", probs, value_rows, preferred_element_type=jnp.float32)
    return (mixture.reshape(seq_len, -1).astype(jnp.bfloat16), row_max + jnp.log(row_total))


def attend_backward(packed):
    queries, key_rows, value_rows, doc_ids, log_total, mix_grad = packed
    seq_len, heads, head_dim = queries.shape
    key_value_heads = key_rows.shape[1]
    grouped, scores = score_block(queries, key_rows, doc_ids)
    probs = jnp.exp(scores - log_total)
    mix_grouped = mix_grad.reshape(seq_len, key_value_heads, heads // key_value_heads, head_dim)
    prob_grad = jnp.einsum(
        "qkgd,tkd->kgqt", mix_grouped, value_rows, preferred_element_type=jnp.float32
    )
    value_grad = jnp.einsum(
        "kgqt,qkgd->tkd",
        probs.astype(jnp.bfloat16),
        mix_grouped,
        preferred_element_type=jnp.float32,
    )
    score_grad = (probs * (prob_grad - jnp.sum(probs * prob_grad, axis=-1, keepdims=True))).astype(
        jnp.bfloat16
    )
    score_scale = head_dim ** (-0.5)
    query_grad = (
        jnp.einsum("kgqt,tkd->qkgd", score_grad, key_rows, preferred_element_type=jnp.float32)
        * score_scale
    )
    key_grad = (
        jnp.einsum("kgqt,qkgd->tkd", score_grad, grouped, preferred_element_type=jnp.float32)
        * score_scale
    )
    return (query_grad.reshape(seq_len, heads, head_dim), key_grad, value_grad.astype(jnp.bfloat16))


def on_device(
    tokens,
    lengths,
    ln_attn,
    w_query,
    w_key,
    w_value,
    q_gain,
    k_gain,
    w_out,
    ln_ffn,
    w_gate,
    w_up,
    w_down,
    out_grad,
):
    parts = lax.axis_size("dp")
    share = w_query.shape[0]
    width = share * parts
    gain_share = q_gain.shape[0]
    head_dim = gain_share * parts
    q_cols, k_cols, v_cols = (w_query.shape[1], w_key.shape[1], w_value.shape[1])
    qkv_cols = q_cols + k_cols + v_cols
    out_rows = w_out.shape[0]
    hidden_units = w_gate.shape[1]
    gain_cols = jnp.stack(
        [
            ln_attn,
            ln_ffn,
            jnp.pad(q_gain, (0, share - gain_share)),
            jnp.pad(k_gain, (0, share - gain_share)),
        ],
        axis=1,
    )
    attn_pack = jnp.concatenate(
        [w_query, w_key, w_value, w_out.T, jnp.pad(gain_cols, ((0, 0), (0, 124)))], axis=1
    )
    attn_all = lax.all_gather(attn_pack, "dp", axis=0, tiled=True)
    tokens_full = lax.all_gather(tokens, "tensor", axis=1, tiled=True)
    qkv_weight = attn_all[:, :qkv_cols]
    out_weight_t = attn_all[:, qkv_cols : qkv_cols + out_rows]
    gains = attn_all[:, qkv_cols + out_rows : qkv_cols + out_rows + 4].astype(jnp.float32)
    attn_gain = gains[:, 0]
    ffn_gain = gains[:, 1]
    query_gain = gains[:, 2].reshape(parts, share)[:, :gain_share].reshape(-1)
    key_gain = gains[:, 3].reshape(parts, share)[:, :gain_share].reshape(-1)
    ffn_pack = jnp.concatenate([w_gate, w_up, w_down.T], axis=1)
    ffn_all = lax.all_gather(ffn_pack, "dp", axis=0, tiled=True)
    gate_up_weight = ffn_all[:, : 2 * hidden_units]
    down_weight_t = ffn_all[:, 2 * hidden_units :]
    grad_full = lax.all_gather(out_grad, "tensor", axis=1, tiled=True)

    inputs = tokens.astype(jnp.float32)
    normed = rms_scale(tokens_full.astype(jnp.float32), attn_gain).astype(jnp.bfloat16)
    seq_count, seq_len = (normed.shape[0], normed.shape[1])
    doc_ids, positions = doc_tables(lengths, seq_len)

    def query_side(raw_heads, gain_vec):
        return rotary(rms_scale(raw_heads, gain_vec), positions)

    qkv_raw = project(normed, qkv_weight)
    query_raw = qkv_raw[..., :q_cols].reshape(seq_count, seq_len, -1, head_dim)
    key_raw = qkv_raw[..., q_cols : q_cols + k_cols].reshape(seq_count, seq_len, -1, head_dim)
    queries = query_side(query_raw, query_gain).astype(jnp.bfloat16)
    key_rows = query_side(key_raw, key_gain).astype(jnp.bfloat16)
    value_rows = (
        qkv_raw[..., q_cols + k_cols :]
        .astype(jnp.bfloat16)
        .reshape(seq_count, seq_len, -1, head_dim)
    )
    mixture, log_total = lax.map(attend_forward, (queries, key_rows, value_rows, doc_ids))
    attn_out = lax.psum_scatter(
        project_back(mixture, out_weight_t).astype(jnp.bfloat16),
        "tensor",
        scatter_dimension=1,
        tiled=True,
    ).astype(jnp.float32)
    mid_stream = inputs + attn_out
    normed_mid = lax.all_gather(
        rms_scale(mid_stream, ffn_gain).astype(jnp.bfloat16),
        "tensor",
        axis=1,
        tiled=True,
    )
    gate_up = project(normed_mid, gate_up_weight)
    gate_proj = gate_up[..., :hidden_units]
    up_proj = gate_up[..., hidden_units:]
    hidden = (jax.nn.silu(gate_proj) * up_proj).astype(jnp.bfloat16)
    hidden_grad = project(grad_full, down_weight_t)
    silu_pull = jax.vjp(
        lambda gate_part, up_part: jax.nn.silu(gate_part) * up_part, gate_proj, up_proj
    )[1]
    gate_grad, up_grad = silu_pull(hidden_grad)
    gate_up_grad = jnp.concatenate([gate_grad, up_grad], axis=-1).astype(jnp.bfloat16)
    mid_norm_grad = lax.psum_scatter(
        project_back(gate_up_grad, gate_up_weight).astype(jnp.bfloat16),
        "tensor",
        scatter_dimension=1,
        tiled=True,
    ).astype(jnp.float32)
    ffn_sums = project_back(hidden, down_weight_t).astype(jnp.bfloat16)
    ffn_w_grads = jnp.concatenate(
        [weight_grad(normed_mid, gate_up_grad), weight_grad(grad_full, hidden)], axis=1
    ).astype(jnp.bfloat16)
    mid_pull = jax.vjp(rms_scale, mid_stream, ffn_gain)[1]
    stream_grad, ffn_gain_grad = mid_pull(mid_norm_grad)
    mid_grad = out_grad.astype(jnp.float32) + stream_grad
    mid_low = lax.all_gather(mid_grad.astype(jnp.bfloat16), "tensor", axis=1, tiled=True)
    mid_low, ffn_w_grads, ffn_sums = lax.optimization_barrier((mid_low, ffn_w_grads, ffn_sums))
    ffn_summed = lax.psum_scatter(ffn_w_grads, "dp", scatter_dimension=0, tiled=True)
    ffn_out = lax.psum_scatter(ffn_sums, "tensor", scatter_dimension=1, tiled=True)
    block_out = (mid_stream + ffn_out.astype(jnp.float32)).astype(jnp.bfloat16)
    out_w_grad_t = weight_grad(mid_low, mixture)
    mix_grad = project(mid_low, out_weight_t).astype(jnp.bfloat16)
    query_grad, key_grad, value_grad = lax.map(
        attend_backward, (queries, key_rows, value_rows, doc_ids, log_total, mix_grad)
    )
    query_pull = jax.vjp(query_side, query_raw, query_gain)[1]
    query_raw_grad, query_gain_grad = query_pull(query_grad)
    key_pull = jax.vjp(query_side, key_raw, key_gain)[1]
    key_raw_grad, key_gain_grad = key_pull(key_grad)
    qkv_low = jnp.concatenate(
        [
            query_raw_grad.reshape(seq_count, seq_len, -1).astype(jnp.bfloat16),
            key_raw_grad.reshape(seq_count, seq_len, -1).astype(jnp.bfloat16),
            value_grad.reshape(seq_count, seq_len, -1),
        ],
        axis=-1,
    )
    input_norm_grad = lax.psum_scatter(
        project_back(qkv_low, qkv_weight).astype(jnp.bfloat16),
        "tensor",
        scatter_dimension=1,
        tiled=True,
    ).astype(jnp.float32)
    input_pull = jax.vjp(rms_scale, inputs, attn_gain)[1]
    input_grad, attn_gain_grad = input_pull(input_norm_grad)
    tokens_grad = mid_grad + input_grad
    gain_cut = jnp.concatenate(
        [
            attn_gain_grad.reshape(parts, share),
            ffn_gain_grad.reshape(parts, share),
            query_gain_grad.reshape(parts, gain_share),
            key_gain_grad.reshape(parts, gain_share),
        ],
        axis=1,
    )
    attn_w_grads = jnp.concatenate(
        [weight_grad(normed, qkv_low), out_w_grad_t], axis=1
    ).astype(jnp.bfloat16)
    attn_summed = lax.psum_scatter(
        attn_w_grads, "dp", scatter_dimension=0, tiled=True
    ).astype(jnp.float32)
    gain_mine = lax.dynamic_index_in_dim(
        lax.psum(gain_cut, ("dp", "tensor")), lax.axis_index("dp"), axis=0, keepdims=False
    )
    ffn_summed = ffn_summed.astype(jnp.float32)
    return (
        block_out,
        tokens_grad,
        gain_mine[:share],
        attn_summed[:, :q_cols],
        attn_summed[:, q_cols : q_cols + k_cols],
        attn_summed[:, q_cols + k_cols : qkv_cols],
        gain_mine[2 * share : 2 * share + gain_share],
        gain_mine[2 * share + gain_share :],
        attn_summed[:, qkv_cols:].T,
        gain_mine[share : 2 * share],
        ffn_summed[:, :hidden_units],
        ffn_summed[:, hidden_units : 2 * hidden_units],
        ffn_summed[:, 2 * hidden_units :].T,
    )


def solution(mesh):
    in_specs = (
        P("dp", "tensor", None),
        P("dp", None),
        P("dp"),
        P("dp", "tensor"),
        P("dp", "tensor"),
        P("dp", "tensor"),
        P("dp"),
        P("dp"),
        P("tensor", "dp"),
        P("dp"),
        P("dp", "tensor"),
        P("dp", "tensor"),
        P("tensor", "dp"),
        P("dp", "tensor", None),
    )
    out_specs = (
        P("dp", "tensor", None),
        P("dp", "tensor", None),
        P("dp"),
        P("dp", "tensor"),
        P("dp", "tensor"),
        P("dp", "tensor"),
        P("dp"),
        P("dp"),
        P("tensor", "dp"),
        P("dp"),
        P("dp", "tensor"),
        P("dp", "tensor"),
        P("tensor", "dp"),
    )
    return jax.shard_map(
        on_device, mesh=mesh, in_specs=in_specs, out_specs=out_specs, check_vma=False
    )
```

```python
import jax
import jax.numpy as jnp
from jax import lax
from jax.sharding import PartitionSpec as P

EPSILON = 1e-05
THETA = 1000000.0
MASKED = -1e30


def rms_scale(values, gain_vec):
    return (
        values * lax.rsqrt(jnp.mean(values * values, axis=-1, keepdims=True) + EPSILON) * gain_vec
    )


def doc_tables(lengths, seq_len):
    doc_ends = jnp.cumsum(lengths, axis=-1, dtype=jnp.int32)
    doc_starts = doc_ends - lengths
    positions = jnp.arange(seq_len, dtype=jnp.int32)
    doc_ids = jnp.sum(
        (positions[None, :, None] >= doc_ends[:, None, :]).astype(jnp.int32),
        axis=-1,
        dtype=jnp.int32,
    )
    numbers = jnp.arange(lengths.shape[-1], dtype=jnp.int32)
    opening = jnp.sum(
        jnp.where(doc_ids[:, :, None] == numbers[None, None, :], doc_starts[:, None, :], 0),
        axis=-1,
        dtype=jnp.int32,
    )
    return (doc_ids, positions[None, :] - opening)


def rotary(values, positions):
    half_dim = values.shape[-1] // 2
    freq_rate = jnp.power(THETA, -2.0 * jnp.arange(half_dim, dtype=jnp.float32) / values.shape[-1])
    angles = positions.astype(jnp.float32)[:, :, None, None] * freq_rate
    cosine = jnp.cos(angles)
    sine_part = jnp.sin(angles)
    front_half = values[..., :half_dim]
    back_half = values[..., half_dim:]
    return jnp.concatenate(
        [front_half * cosine - back_half * sine_part, back_half * cosine + front_half * sine_part],
        axis=-1,
    )


def allowed_mask(doc_ids):
    places = jnp.arange(doc_ids.shape[0], dtype=jnp.int32)
    return (doc_ids[:, None] == doc_ids[None, :]) & (places[None, :] <= places[:, None])


def project(matmul_operand, weight_matrix):
    return jnp.einsum(
        "xpo,oh->xph", matmul_operand, weight_matrix, preferred_element_type=jnp.float32
    )


def project_back(gradient_term, weight_matrix):
    return jnp.einsum(
        "yhp,np->yhn", gradient_term, weight_matrix, preferred_element_type=jnp.float32
    )


def weight_grad(matmul_operand, gradient_term):
    return jnp.einsum(
        "wba,wbh->ah", matmul_operand, gradient_term, preferred_element_type=jnp.float32
    )


def score_block(queries, key_rows, doc_ids):
    seq_len, heads, head_dim = queries.shape
    key_value_heads = key_rows.shape[1]
    grouped = queries.reshape(seq_len, key_value_heads, heads // key_value_heads, head_dim)
    scores = jnp.einsum(
        "qkgd,tkd->kgqt", grouped, key_rows, preferred_element_type=jnp.float32
    ) * head_dim ** (-0.5)
    return (grouped, jnp.where(allowed_mask(doc_ids), scores, MASKED))


def attend_forward(packed):
    queries, key_rows, value_rows, doc_ids = packed
    seq_len = queries.shape[0]
    grouped, scores = score_block(queries, key_rows, doc_ids)
    row_max = jnp.max(scores, axis=-1, keepdims=True)
    exp_scores = jnp.exp(scores - row_max)
    row_total = jnp.sum(exp_scores, axis=-1, keepdims=True)
    probs = (exp_scores / row_total).astype(jnp.bfloat16)
    mixture = jnp.einsum("kgqt,tkd->qkgd", probs, value_rows, preferred_element_type=jnp.float32)
    return (mixture.reshape(seq_len, -1).astype(jnp.bfloat16), row_max + jnp.log(row_total))


def attend_backward(packed):
    queries, key_rows, value_rows, doc_ids, log_total, mix_grad = packed
    seq_len, heads, head_dim = queries.shape
    key_value_heads = key_rows.shape[1]
    grouped, scores = score_block(queries, key_rows, doc_ids)
    probs = jnp.exp(scores - log_total)
    mix_grouped = mix_grad.reshape(seq_len, key_value_heads, heads // key_value_heads, head_dim)
    prob_grad = jnp.einsum(
        "qkgd,tkd->kgqt", mix_grouped, value_rows, preferred_element_type=jnp.float32
    )
    value_grad = jnp.einsum(
        "kgqt,qkgd->tkd",
        probs.astype(jnp.bfloat16),
        mix_grouped,
        preferred_element_type=jnp.float32,
    )
    score_grad = (probs * (prob_grad - jnp.sum(probs * prob_grad, axis=-1, keepdims=True))).astype(
        jnp.bfloat16
    )
    score_scale = head_dim ** (-0.5)
    query_grad = (
        jnp.einsum("kgqt,tkd->qkgd", score_grad, key_rows, preferred_element_type=jnp.float32)
        * score_scale
    )
    key_grad = (
        jnp.einsum("kgqt,qkgd->tkd", score_grad, grouped, preferred_element_type=jnp.float32)
        * score_scale
    )
    return (query_grad.reshape(seq_len, heads, head_dim), key_grad, value_grad.astype(jnp.bfloat16))


def each_sequence(attend, packed):
    results = [
        attend(tuple(part[index] for part in packed)) for index in range(packed[0].shape[0])
    ]
    return tuple(jnp.stack(parts) for parts in zip(*results))


def on_device(
    tokens,
    lengths,
    ln_attn,
    w_query,
    w_key,
    w_value,
    q_gain,
    k_gain,
    w_out,
    ln_ffn,
    w_gate,
    w_up,
    w_down,
    out_grad,
):
    parts = lax.axis_size("dp")
    share = w_query.shape[0]
    width = share * parts
    gain_share = q_gain.shape[0]
    head_dim = gain_share * parts
    q_cols, k_cols, v_cols = (w_query.shape[1], w_key.shape[1], w_value.shape[1])
    qkv_cols = q_cols + k_cols + v_cols
    out_rows = w_out.shape[0]
    hidden_units = w_gate.shape[1]
    gain_cols = jnp.stack(
        [
            ln_attn,
            ln_ffn,
            jnp.pad(q_gain, (0, share - gain_share)),
            jnp.pad(k_gain, (0, share - gain_share)),
        ],
        axis=1,
    )
    attn_pack = jnp.concatenate(
        [w_query, w_key, w_value, w_out.T, jnp.pad(gain_cols, ((0, 0), (0, 124)))], axis=1
    )
    attn_all = lax.all_gather(attn_pack, "dp", axis=0, tiled=True)
    tokens_full = lax.all_gather(tokens, "tensor", axis=1, tiled=True)
    qkv_weight = attn_all[:, :qkv_cols]
    out_weight_t = attn_all[:, qkv_cols : qkv_cols + out_rows]
    gains = attn_all[:, qkv_cols + out_rows : qkv_cols + out_rows + 4].astype(jnp.float32)
    attn_gain = gains[:, 0]
    ffn_gain = gains[:, 1]
    query_gain = gains[:, 2].reshape(parts, share)[:, :gain_share].reshape(-1)
    key_gain = gains[:, 3].reshape(parts, share)[:, :gain_share].reshape(-1)
    gate_up_weight = lax.all_gather(
        jnp.concatenate([w_gate, w_up], axis=1), "dp", axis=0, tiled=True
    )
    down_weight_t = lax.all_gather(w_down.T, "dp", axis=0, tiled=True)
    grad_full = lax.all_gather(out_grad, "tensor", axis=1, tiled=True)

    inputs = tokens.astype(jnp.float32)
    normed = rms_scale(tokens_full.astype(jnp.float32), attn_gain).astype(jnp.bfloat16)
    seq_count, seq_len = (normed.shape[0], normed.shape[1])
    doc_ids, positions = doc_tables(lengths, seq_len)

    def query_side(raw_heads, gain_vec):
        return rotary(rms_scale(raw_heads, gain_vec), positions)

    qkv_raw = project(normed, qkv_weight)
    query_raw = qkv_raw[..., :q_cols].reshape(seq_count, seq_len, -1, head_dim)
    key_raw = qkv_raw[..., q_cols : q_cols + k_cols].reshape(seq_count, seq_len, -1, head_dim)
    queries = query_side(query_raw, query_gain).astype(jnp.bfloat16)
    key_rows = query_side(key_raw, key_gain).astype(jnp.bfloat16)
    value_rows = (
        qkv_raw[..., q_cols + k_cols :]
        .astype(jnp.bfloat16)
        .reshape(seq_count, seq_len, -1, head_dim)
    )
    mixture, log_total = each_sequence(attend_forward, (queries, key_rows, value_rows, doc_ids))
    attn_sums = project_back(mixture, out_weight_t).astype(jnp.bfloat16)
    attn_sums, gate_up_weight = lax.optimization_barrier((attn_sums, gate_up_weight))
    attn_out = lax.psum_scatter(
        attn_sums,
        "tensor",
        scatter_dimension=1,
        tiled=True,
    ).astype(jnp.float32)
    mid_stream = inputs + attn_out
    normed_mine = rms_scale(mid_stream, ffn_gain).astype(jnp.bfloat16)
    normed_mine, down_weight_t = lax.optimization_barrier((normed_mine, down_weight_t))
    normed_mid = lax.all_gather(normed_mine, "tensor", axis=1, tiled=True)
    gate_up = project(normed_mid, gate_up_weight)
    gate_proj = gate_up[..., :hidden_units]
    up_proj = gate_up[..., hidden_units:]
    hidden = (jax.nn.silu(gate_proj) * up_proj).astype(jnp.bfloat16)
    hidden_grad = project(grad_full, down_weight_t)
    silu_pull = jax.vjp(
        lambda gate_part, up_part: jax.nn.silu(gate_part) * up_part, gate_proj, up_proj
    )[1]
    gate_grad, up_grad = silu_pull(hidden_grad)
    gate_up_grad = jnp.concatenate([gate_grad, up_grad], axis=-1).astype(jnp.bfloat16)
    mid_norm_grad = lax.psum_scatter(
        project_back(gate_up_grad, gate_up_weight).astype(jnp.bfloat16),
        "tensor",
        scatter_dimension=1,
        tiled=True,
    ).astype(jnp.float32)
    ffn_sums = project_back(hidden, down_weight_t).astype(jnp.bfloat16)
    ffn_w_grads = jnp.concatenate(
        [weight_grad(normed_mid, gate_up_grad), weight_grad(grad_full, hidden)], axis=1
    ).astype(jnp.bfloat16)
    mid_pull = jax.vjp(rms_scale, mid_stream, ffn_gain)[1]
    stream_grad, ffn_gain_grad = mid_pull(mid_norm_grad)
    mid_grad = out_grad.astype(jnp.float32) + stream_grad
    mid_low = lax.all_gather(mid_grad.astype(jnp.bfloat16), "tensor", axis=1, tiled=True)
    mid_low, ffn_w_grads = lax.optimization_barrier((mid_low, ffn_w_grads))
    ffn_summed = lax.psum_scatter(ffn_w_grads, "dp", scatter_dimension=0, tiled=True)
    ffn_out = lax.psum_scatter(ffn_sums, "tensor", scatter_dimension=1, tiled=True)
    out_w_grad_t = weight_grad(mid_low, mixture)
    mix_grad = project(mid_low, out_weight_t).astype(jnp.bfloat16)
    query_grad, key_grad, value_grad = each_sequence(
        attend_backward, (queries, key_rows, value_rows, doc_ids, log_total, mix_grad)
    )
    query_pull = jax.vjp(query_side, query_raw, query_gain)[1]
    query_raw_grad, query_gain_grad = query_pull(query_grad)
    key_pull = jax.vjp(query_side, key_raw, key_gain)[1]
    key_raw_grad, key_gain_grad = key_pull(key_grad)
    qkv_low = jnp.concatenate(
        [
            query_raw_grad.reshape(seq_count, seq_len, -1).astype(jnp.bfloat16),
            key_raw_grad.reshape(seq_count, seq_len, -1).astype(jnp.bfloat16),
            value_grad.reshape(seq_count, seq_len, -1),
        ],
        axis=-1,
    )
    qkv_low, ffn_summed, ffn_out = lax.optimization_barrier((qkv_low, ffn_summed, ffn_out))
    block_out = (mid_stream + ffn_out.astype(jnp.float32)).astype(jnp.bfloat16)
    input_sums = project_back(qkv_low, qkv_weight)
    attn_gain_grad = jnp.sum(
        input_sums * rms_scale(tokens_full.astype(jnp.float32), 1.0), axis=(0, 1)
    )
    input_norm_grad = lax.psum_scatter(
        input_sums.astype(jnp.bfloat16),
        "tensor",
        scatter_dimension=1,
        tiled=True,
    ).astype(jnp.float32)
    input_pull = jax.vjp(rms_scale, inputs, attn_gain)[1]
    input_grad = input_pull(input_norm_grad)[0]
    tokens_grad = mid_grad + input_grad
    gain_cut = jnp.concatenate(
        [
            attn_gain_grad.reshape(parts, share),
            ffn_gain_grad.reshape(parts, share),
            query_gain_grad.reshape(parts, gain_share),
            key_gain_grad.reshape(parts, gain_share),
        ],
        axis=1,
    )
    attn_w_grads = jnp.concatenate(
        [weight_grad(normed, qkv_low), out_w_grad_t], axis=1
    ).astype(jnp.bfloat16)
    attn_summed = lax.psum_scatter(
        attn_w_grads, "dp", scatter_dimension=0, tiled=True
    ).astype(jnp.float32)
    gain_mine = lax.dynamic_index_in_dim(
        lax.psum(gain_cut, ("dp", "tensor")), lax.axis_index("dp"), axis=0, keepdims=False
    )
    ffn_summed = ffn_summed.astype(jnp.float32)
    return (
        block_out,
        tokens_grad,
        gain_mine[:share],
        attn_summed[:, :q_cols],
        attn_summed[:, q_cols : q_cols + k_cols],
        attn_summed[:, q_cols + k_cols : qkv_cols],
        gain_mine[2 * share : 2 * share + gain_share],
        gain_mine[2 * share + gain_share :],
        attn_summed[:, qkv_cols:].T,
        gain_mine[share : 2 * share],
        ffn_summed[:, :hidden_units],
        ffn_summed[:, hidden_units : 2 * hidden_units],
        ffn_summed[:, 2 * hidden_units :].T,
    )


def solution(mesh):
    in_specs = (
        P("dp", "tensor", None),
        P("dp", None),
        P("dp"),
        P("dp", "tensor"),
        P("dp", "tensor"),
        P("dp", "tensor"),
        P("dp"),
        P("dp"),
        P("tensor", "dp"),
        P("dp"),
        P("dp", "tensor"),
        P("dp", "tensor"),
        P("tensor", "dp"),
        P("dp", "tensor", None),
    )
    out_specs = (
        P("dp", "tensor", None),
        P("dp", "tensor", None),
        P("dp"),
        P("dp", "tensor"),
        P("dp", "tensor"),
        P("dp", "tensor"),
        P("dp"),
        P("dp"),
        P("tensor", "dp"),
        P("dp"),
        P("dp", "tensor"),
        P("dp", "tensor"),
        P("tensor", "dp"),
    )
    return jax.shard_map(
        on_device, mesh=mesh, in_specs=in_specs, out_specs=out_specs, check_vma=False
    )
```

```python
import jax
import jax.numpy as jnp
from jax import lax
from jax.sharding import PartitionSpec as P

EPSILON = 1e-05
THETA = 1000000.0
MASKED = -1e30


def rms_scale(values, gain_vec):
    return (
        values * lax.rsqrt(jnp.mean(values * values, axis=-1, keepdims=True) + EPSILON) * gain_vec
    )


def doc_tables(lengths, seq_len):
    doc_ends = jnp.cumsum(lengths, axis=-1, dtype=jnp.int32)
    doc_starts = doc_ends - lengths
    positions = jnp.arange(seq_len, dtype=jnp.int32)
    doc_ids = jnp.sum(
        (positions[None, :, None] >= doc_ends[:, None, :]).astype(jnp.int32),
        axis=-1,
        dtype=jnp.int32,
    )
    numbers = jnp.arange(lengths.shape[-1], dtype=jnp.int32)
    opening = jnp.sum(
        jnp.where(doc_ids[:, :, None] == numbers[None, None, :], doc_starts[:, None, :], 0),
        axis=-1,
        dtype=jnp.int32,
    )
    return (doc_ids, positions[None, :] - opening)


def rotary(values, positions):
    half_dim = values.shape[-1] // 2
    freq_rate = jnp.power(THETA, -2.0 * jnp.arange(half_dim, dtype=jnp.float32) / values.shape[-1])
    angles = positions.astype(jnp.float32)[:, :, None, None] * freq_rate
    cosine = jnp.cos(angles)
    sine_part = jnp.sin(angles)
    front_half = values[..., :half_dim]
    back_half = values[..., half_dim:]
    return jnp.concatenate(
        [front_half * cosine - back_half * sine_part, back_half * cosine + front_half * sine_part],
        axis=-1,
    )


def allowed_mask(doc_ids):
    places = jnp.arange(doc_ids.shape[0], dtype=jnp.int32)
    return (doc_ids[:, None] == doc_ids[None, :]) & (places[None, :] <= places[:, None])


def project(matmul_operand, weight_matrix):
    return jnp.einsum(
        "xpo,oh->xph", matmul_operand, weight_matrix, preferred_element_type=jnp.float32
    )


def project_back(gradient_term, weight_matrix):
    return jnp.einsum(
        "yhp,np->yhn", gradient_term, weight_matrix, preferred_element_type=jnp.float32
    )


def weight_grad(matmul_operand, gradient_term):
    return jnp.einsum(
        "wba,wbh->ah", matmul_operand, gradient_term, preferred_element_type=jnp.float32
    )


def score_block(queries, key_rows, doc_ids):
    seq_len, heads, head_dim = queries.shape
    key_value_heads = key_rows.shape[1]
    grouped = queries.reshape(seq_len, key_value_heads, heads // key_value_heads, head_dim)
    scores = jnp.einsum(
        "qkgd,tkd->kgqt", grouped, key_rows, preferred_element_type=jnp.float32
    ) * head_dim ** (-0.5)
    return (grouped, jnp.where(allowed_mask(doc_ids), scores, MASKED))


def attend_forward(packed):
    queries, key_rows, value_rows, doc_ids = packed
    seq_len = queries.shape[0]
    grouped, scores = score_block(queries, key_rows, doc_ids)
    row_max = jnp.max(scores, axis=-1, keepdims=True)
    exp_scores = jnp.exp(scores - row_max)
    row_total = jnp.sum(exp_scores, axis=-1, keepdims=True)
    probs = (exp_scores / row_total).astype(jnp.bfloat16)
    mixture = jnp.einsum("kgqt,tkd->qkgd", probs, value_rows, preferred_element_type=jnp.float32)
    return (mixture.reshape(seq_len, -1).astype(jnp.bfloat16), row_max + jnp.log(row_total))


def attend_backward(packed):
    queries, key_rows, value_rows, doc_ids, log_total, mix_grad = packed
    seq_len, heads, head_dim = queries.shape
    key_value_heads = key_rows.shape[1]
    grouped, scores = score_block(queries, key_rows, doc_ids)
    probs = jnp.exp(scores - log_total)
    mix_grouped = mix_grad.reshape(seq_len, key_value_heads, heads // key_value_heads, head_dim)
    prob_grad = jnp.einsum(
        "qkgd,tkd->kgqt", mix_grouped, value_rows, preferred_element_type=jnp.float32
    )
    value_grad = jnp.einsum(
        "kgqt,qkgd->tkd",
        probs.astype(jnp.bfloat16),
        mix_grouped,
        preferred_element_type=jnp.float32,
    )
    score_grad = (probs * (prob_grad - jnp.sum(probs * prob_grad, axis=-1, keepdims=True))).astype(
        jnp.bfloat16
    )
    score_scale = head_dim ** (-0.5)
    query_grad = (
        jnp.einsum("kgqt,tkd->qkgd", score_grad, key_rows, preferred_element_type=jnp.float32)
        * score_scale
    )
    key_grad = (
        jnp.einsum("kgqt,qkgd->tkd", score_grad, grouped, preferred_element_type=jnp.float32)
        * score_scale
    )
    return (query_grad.reshape(seq_len, heads, head_dim), key_grad, value_grad.astype(jnp.bfloat16))


def shifted(block, step):
    parts = lax.axis_size("tensor")
    return lax.ppermute(block, "tensor", [(place, (place + step) % parts) for place in range(parts)])


def gather_positions(mine):
    parts = lax.axis_size("tensor")
    place = lax.axis_index("tensor")
    rows = mine.shape[1]
    whole = jnp.zeros((mine.shape[0], rows * parts, mine.shape[2]), mine.dtype)
    for step in range(parts):
        piece = mine if step == 0 else shifted(mine, step)
        whole = lax.dynamic_update_slice_in_dim(
            whole, piece, ((place + parts - step) % parts) * rows, axis=1
        )
    return whole


def scatter_positions(sums):
    parts = lax.axis_size("tensor")
    place = lax.axis_index("tensor")
    rows = sums.shape[1] // parts
    total = None
    for step in range(parts):
        piece = lax.dynamic_slice_in_dim(sums, ((place + step) % parts) * rows, rows, axis=1)
        piece = piece if step == 0 else shifted(piece, step)
        piece = piece.astype(jnp.float32)
        total = piece if total is None else total + piece
    return total


def each_sequence(attend, packed):
    results = [
        attend(tuple(part[index] for part in packed)) for index in range(packed[0].shape[0])
    ]
    return tuple(jnp.stack(parts) for parts in zip(*results))


def on_device(
    tokens,
    lengths,
    ln_attn,
    w_query,
    w_key,
    w_value,
    q_gain,
    k_gain,
    w_out,
    ln_ffn,
    w_gate,
    w_up,
    w_down,
    out_grad,
):
    parts = lax.axis_size("dp")
    share = w_query.shape[0]
    width = share * parts
    gain_share = q_gain.shape[0]
    head_dim = gain_share * parts
    q_cols, k_cols, v_cols = (w_query.shape[1], w_key.shape[1], w_value.shape[1])
    qkv_cols = q_cols + k_cols + v_cols
    out_rows = w_out.shape[0]
    hidden_units = w_gate.shape[1]
    gain_cols = jnp.stack(
        [
            ln_attn,
            ln_ffn,
            jnp.pad(q_gain, (0, share - gain_share)),
            jnp.pad(k_gain, (0, share - gain_share)),
        ],
        axis=1,
    )
    attn_pack = jnp.concatenate(
        [w_query, w_key, w_value, w_out.T, jnp.pad(gain_cols, ((0, 0), (0, 124)))], axis=1
    )
    attn_all = lax.all_gather(attn_pack, "dp", axis=0, tiled=True)
    tokens_full = gather_positions(tokens)
    qkv_weight = attn_all[:, :qkv_cols]
    out_weight_t = attn_all[:, qkv_cols : qkv_cols + out_rows]
    gains = attn_all[:, qkv_cols + out_rows : qkv_cols + out_rows + 4].astype(jnp.float32)
    attn_gain = gains[:, 0]
    ffn_gain = gains[:, 1]
    query_gain = gains[:, 2].reshape(parts, share)[:, :gain_share].reshape(-1)
    key_gain = gains[:, 3].reshape(parts, share)[:, :gain_share].reshape(-1)
    gate_up_weight = lax.all_gather(
        jnp.concatenate([w_gate, w_up], axis=1), "dp", axis=0, tiled=True
    )
    down_weight_t = lax.all_gather(w_down.T, "dp", axis=0, tiled=True)
    grad_full = gather_positions(out_grad)

    inputs = tokens.astype(jnp.float32)
    normed = rms_scale(tokens_full.astype(jnp.float32), attn_gain).astype(jnp.bfloat16)
    seq_count, seq_len = (normed.shape[0], normed.shape[1])
    doc_ids, positions = doc_tables(lengths, seq_len)

    def query_side(raw_heads, gain_vec):
        return rotary(rms_scale(raw_heads, gain_vec), positions)

    qkv_raw = project(normed, qkv_weight)
    query_raw = qkv_raw[..., :q_cols].reshape(seq_count, seq_len, -1, head_dim)
    key_raw = qkv_raw[..., q_cols : q_cols + k_cols].reshape(seq_count, seq_len, -1, head_dim)
    queries = query_side(query_raw, query_gain).astype(jnp.bfloat16)
    key_rows = query_side(key_raw, key_gain).astype(jnp.bfloat16)
    value_rows = (
        qkv_raw[..., q_cols + k_cols :]
        .astype(jnp.bfloat16)
        .reshape(seq_count, seq_len, -1, head_dim)
    )
    mixture, log_total = each_sequence(attend_forward, (queries, key_rows, value_rows, doc_ids))
    attn_sums = project_back(mixture, out_weight_t).astype(jnp.bfloat16)
    attn_sums, gate_up_weight = lax.optimization_barrier((attn_sums, gate_up_weight))
    attn_out = scatter_positions(attn_sums)
    mid_stream = inputs + attn_out
    normed_mine = rms_scale(mid_stream, ffn_gain).astype(jnp.bfloat16)
    normed_mine, down_weight_t = lax.optimization_barrier((normed_mine, down_weight_t))
    normed_mid = lax.all_gather(normed_mine, "tensor", axis=1, tiled=True)
    gate_up = project(normed_mid, gate_up_weight)
    gate_proj = gate_up[..., :hidden_units]
    up_proj = gate_up[..., hidden_units:]
    hidden = (jax.nn.silu(gate_proj) * up_proj).astype(jnp.bfloat16)
    hidden_grad = project(grad_full, down_weight_t)
    silu_pull = jax.vjp(
        lambda gate_part, up_part: jax.nn.silu(gate_part) * up_part, gate_proj, up_proj
    )[1]
    gate_grad, up_grad = silu_pull(hidden_grad)
    gate_up_grad = jnp.concatenate([gate_grad, up_grad], axis=-1).astype(jnp.bfloat16)
    mid_norm_grad = lax.psum_scatter(
        project_back(gate_up_grad, gate_up_weight).astype(jnp.bfloat16),
        "tensor",
        scatter_dimension=1,
        tiled=True,
    ).astype(jnp.float32)
    ffn_sums = project_back(hidden, down_weight_t).astype(jnp.bfloat16)
    ffn_w_grads = jnp.concatenate(
        [weight_grad(normed_mid, gate_up_grad), weight_grad(grad_full, hidden)], axis=1
    ).astype(jnp.bfloat16)
    mid_pull = jax.vjp(rms_scale, mid_stream, ffn_gain)[1]
    stream_grad, ffn_gain_grad = mid_pull(mid_norm_grad)
    mid_grad = out_grad.astype(jnp.float32) + stream_grad
    mid_low = lax.all_gather(mid_grad.astype(jnp.bfloat16), "tensor", axis=1, tiled=True)
    mid_low, ffn_w_grads = lax.optimization_barrier((mid_low, ffn_w_grads))
    ffn_summed = lax.psum_scatter(ffn_w_grads, "dp", scatter_dimension=0, tiled=True)
    ffn_out = scatter_positions(ffn_sums)
    out_w_grad_t = weight_grad(mid_low, mixture)
    mix_grad = project(mid_low, out_weight_t).astype(jnp.bfloat16)
    query_grad, key_grad, value_grad = each_sequence(
        attend_backward, (queries, key_rows, value_rows, doc_ids, log_total, mix_grad)
    )
    query_pull = jax.vjp(query_side, query_raw, query_gain)[1]
    query_raw_grad, query_gain_grad = query_pull(query_grad)
    key_pull = jax.vjp(query_side, key_raw, key_gain)[1]
    key_raw_grad, key_gain_grad = key_pull(key_grad)
    qkv_low = jnp.concatenate(
        [
            query_raw_grad.reshape(seq_count, seq_len, -1).astype(jnp.bfloat16),
            key_raw_grad.reshape(seq_count, seq_len, -1).astype(jnp.bfloat16),
            value_grad.reshape(seq_count, seq_len, -1),
        ],
        axis=-1,
    )
    qkv_low, ffn_summed, ffn_out = lax.optimization_barrier((qkv_low, ffn_summed, ffn_out))
    block_out = (mid_stream + ffn_out).astype(jnp.bfloat16)
    input_sums = project_back(qkv_low, qkv_weight)
    attn_gain_grad = jnp.sum(
        input_sums * rms_scale(tokens_full.astype(jnp.float32), 1.0), axis=(0, 1)
    )
    input_norm_grad = scatter_positions(input_sums.astype(jnp.bfloat16))
    input_pull = jax.vjp(rms_scale, inputs, attn_gain)[1]
    input_grad = input_pull(input_norm_grad)[0]
    tokens_grad = mid_grad + input_grad
    gain_cut = jnp.concatenate(
        [
            attn_gain_grad.reshape(parts, share),
            ffn_gain_grad.reshape(parts, share),
            query_gain_grad.reshape(parts, gain_share),
            key_gain_grad.reshape(parts, gain_share),
        ],
        axis=1,
    )
    attn_w_grads = jnp.concatenate(
        [weight_grad(normed, qkv_low), out_w_grad_t], axis=1
    ).astype(jnp.bfloat16)
    attn_summed = lax.psum_scatter(
        attn_w_grads, "dp", scatter_dimension=0, tiled=True
    ).astype(jnp.float32)
    gain_mine = lax.dynamic_index_in_dim(
        lax.psum(gain_cut, ("dp", "tensor")), lax.axis_index("dp"), axis=0, keepdims=False
    )
    ffn_summed = ffn_summed.astype(jnp.float32)
    return (
        block_out,
        tokens_grad,
        gain_mine[:share],
        attn_summed[:, :q_cols],
        attn_summed[:, q_cols : q_cols + k_cols],
        attn_summed[:, q_cols + k_cols : qkv_cols],
        gain_mine[2 * share : 2 * share + gain_share],
        gain_mine[2 * share + gain_share :],
        attn_summed[:, qkv_cols:].T,
        gain_mine[share : 2 * share],
        ffn_summed[:, :hidden_units],
        ffn_summed[:, hidden_units : 2 * hidden_units],
        ffn_summed[:, 2 * hidden_units :].T,
    )


def solution(mesh):
    in_specs = (
        P("dp", "tensor", None),
        P("dp", None),
        P("dp"),
        P("dp", "tensor"),
        P("dp", "tensor"),
        P("dp", "tensor"),
        P("dp"),
        P("dp"),
        P("tensor", "dp"),
        P("dp"),
        P("dp", "tensor"),
        P("dp", "tensor"),
        P("tensor", "dp"),
        P("dp", "tensor", None),
    )
    out_specs = (
        P("dp", "tensor", None),
        P("dp", "tensor", None),
        P("dp"),
        P("dp", "tensor"),
        P("dp", "tensor"),
        P("dp", "tensor"),
        P("dp"),
        P("dp"),
        P("tensor", "dp"),
        P("dp"),
        P("dp", "tensor"),
        P("dp", "tensor"),
        P("tensor", "dp"),
    )
    return jax.shard_map(
        on_device, mesh=mesh, in_specs=in_specs, out_specs=out_specs, check_vma=False
    )
```
